32 devices in a mesh: fsdp: 32 (over z, y, x, core).
Axes of the slice: x: 2, y: 2, z: 4, core: 2. Of those that a mesh axis runs over, the one named last changes fastest.
Arguments:
- tokens: bfloat16 [65536, 768], P('fsdp'), may hold values from -6 to 6
- seq_lengths: int32 [32, 2, 4], P('fsdp'), may hold values from 0 to 1024, as said below
- query_weight: bfloat16 [768, 768], P('fsdp'), may hold values from -0.21875 to 0.21875
- query_bias: bfloat16 [768], P('fsdp'), may hold values from -3 to 3
- key_weight: bfloat16 [768, 768], P('fsdp'), may hold values from -0.21875 to 0.21875
- value_weight: bfloat16 [768, 768], P('fsdp'), may hold values from -0.21875 to 0.21875
- value_bias: bfloat16 [768], P('fsdp'), may hold values from -3 to 3
- output_weight: bfloat16 [768, 768], P('fsdp'), may hold values from -0.875 to 0.875
- output_bias: bfloat16 [768], P('fsdp'), may hold values from -3 to 3
- first_gain: bfloat16 [768], P('fsdp'), may hold values from 0.099609375 to 1.8984375
- first_shift: bfloat16 [768], P('fsdp'), may hold values from -3 to 3
- up_weight: bfloat16 [768, 3072], P('fsdp'), may hold values from -0.21875 to 0.21875
- up_bias: bfloat16 [3072], P('fsdp'), may hold values from -3 to 3
- down_weight: bfloat16 [3072, 768], P('fsdp'), may hold values from -0.109375 to 0.109375
- down_bias: bfloat16 [768], P('fsdp'), may hold values from -3 to 3
- second_gain: bfloat16 [768], P('fsdp'), may hold values from 0.099609375 to 1.8984375
- second_shift: bfloat16 [768], P('fsdp'), may hold values from -3 to 3
- cotangent: bfloat16 [65536, 768], P('fsdp'), may hold values from -6 to 6
Outputs:
- layer_output: bfloat16 [65536, 768], P('fsdp')
- token_gradient: float32 [65536, 768], P('fsdp')
- query_weight_gradient: float32 [768, 768], P('fsdp')
- query_bias_gradient: float32 [768], P('fsdp')
- key_weight_gradient: float32 [768, 768], P('fsdp')
- value_weight_gradient: float32 [768, 768], P('fsdp')
- value_bias_gradient: float32 [768], P('fsdp')
- output_weight_gradient: float32 [768, 768], P('fsdp')
- output_bias_gradient: float32 [768], P('fsdp')
- first_gain_gradient: float32 [768], P('fsdp')
- first_shift_gradient: float32 [768], P('fsdp')
- up_weight_gradient: float32 [768, 3072], P('fsdp')
- up_bias_gradient: float32 [3072], P('fsdp')
- down_weight_gradient: float32 [3072, 768], P('fsdp')
- down_bias_gradient: float32 [768], P('fsdp')
- second_gain_gradient: float32 [768], P('fsdp')
- second_shift_gradient: float32 [768], P('fsdp')
The draws below stay inside these ranges and needn't reach their ends.
Inputs may be any that keep to these rules, and one draw needn't show every extreme that they name: Each row seq_lengths[d, m, :] lists, in order, the sequences packed into slot m of device d: either one sequence of exactly 1024 tokens followed by zeros, or 4 sequences of 128 to 256 tokens each, or all zeros for an unused slot. A device's used slots come first and it uses 1 to 2 of them; some slot holds a sequence of exactly 1024 tokens and some device uses all 2 slots.
All inputs are finite; a program needn't handle non-finite values.
Results may differ from the reference program's by a relative error of at most 0.014.
Values may be sent and summed in bfloat16 or wider, within the bound.
A program may use at most 192 MiB of HBM per device.

```python
import jax
import jax.numpy as jnp
from jax import lax

D = 768
H = 12
HD = 64
FF = 3072
MBS = 2
MBLEN = 1024
PACK = 4
TOKENS = 65536
DEVICES = 32


def draw_seq_lengths(key, part):
    key = jax.random.fold_in(key, 11)
    keys = jax.random.split(key, 4)
    short = jax.random.randint(keys[0], (DEVICES, MBS, PACK), MBLEN // (2 * PACK), MBLEN // PACK + 1)
    whole_pick = jax.random.randint(keys[1], (DEVICES, MBS), 0, 4)
    counts = jax.random.randint(keys[2], (DEVICES,), 1, MBS + 1)
    chosen = jax.random.randint(keys[3], (), 0, DEVICES)
    device_ids = jnp.arange(DEVICES, dtype=jnp.int32)
    slot_ids = jnp.arange(MBS, dtype=jnp.int32)
    counts = jnp.where(device_ids == (chosen + 1) % DEVICES, MBS, counts)
    whole = (whole_pick == 0) | (device_ids[:, None] == chosen) & (slot_ids[None, :] == 0)
    single = jnp.where(jnp.arange(PACK, dtype=jnp.int32) == 0, MBLEN, 0)
    lengths = jnp.where(whole[:, :, None], single[None, None, :], short)
    used = slot_ids[None, :] < counts[:, None]
    return jnp.where(used[:, :, None], lengths, 0).astype(jnp.int32)


def strengthened(values, rng, source, target, shards_of, factor):
    def block_of(position):
        return (jnp.arange(values.shape[position]) // (values.shape[position] // shards_of)).reshape((-1,) + (1,) * (values.ndim - 1 - position))

    one_side = jax.random.permutation(rng, shards_of)[block_of(target)]
    second = (block_of(target) + shards_of // 2) % shards_of
    return jnp.where((block_of(source) == one_side) | (block_of(source) == second), factor * values, values)


def block_levels(own_key, shape, cuts, smallest, top_value):
    level, own = 1.0, jax.random.fold_in(own_key, 6)
    for axis_at, shards_of in cuts:
        heights = jnp.exp(jax.random.uniform(jax.random.fold_in(own, axis_at), (shards_of,), jnp.float32, smallest / len(cuts), top_value / len(cuts)))
        level = level * jnp.repeat(heights, shape[axis_at] // shards_of).reshape([-1 if axis == axis_at else 1 for axis in range(len(shape))])
    return level


def bell_draw(own_key, shape, deviation, bound, pieces=(), kind=jnp.bfloat16):
    values = jax.random.normal(own_key, shape, jnp.float32) * deviation
    if len(pieces) > 0:
        values = block_levels(own_key, shape, pieces, -0.22, 0.18) * values
    return jnp.clip(values, min=-bound, max=bound).astype(kind)


def heavy_noise(own_key, dims, spread, most, pieces, heavy, held_as=jnp.bfloat16):
    values = spread * jax.random.normal(own_key, dims, jnp.float32)
    if pieces:
        values = values * block_levels(own_key, dims, pieces, -0.22, 0.18)
    return jnp.clip(strengthened(values, jax.random.fold_in(own_key, 3), *heavy), -most, most).astype(held_as)


def setup_inputs(seed: int = 0) -> dict:
    splits = jax.random.split(jax.random.key(seed), 19)
    tokens = bell_draw(splits[0], (TOKENS, D), 1.0, 6.0, ((0, 32),))
    seq_lengths = draw_seq_lengths(jax.random.fold_in(splits[18], 71), 0)
    query_weight = bell_draw(splits[2], (D, D), D ** -0.5, 0.21875, ((0, 32),))
    query_bias = bell_draw(splits[3], (D,), 0.5, 3.0, ((0, 32),))
    key_weight = bell_draw(splits[4], (D, D), D ** -0.5, 0.21875, ((0, 32),))
    value_weight = bell_draw(splits[5], (D, D), D ** -0.5, 0.21875, ((0, 32),))
    value_bias = bell_draw(splits[6], (D,), 0.5, 3.0, ((0, 32),))
    output_weight = bell_draw(splits[7], (D, D), (D // 16) ** -0.5, 0.875, ((0, 32),))
    output_bias = bell_draw(splits[8], (D,), 0.5, 3.0, ((0, 32),))
    first_gain = jnp.clip(1.0 + 0.18 * jax.random.normal(splits[9], (D,), jnp.float32), 0.099609375, 1.8984375).astype(jnp.bfloat16)
    first_shift = bell_draw(splits[10], (D,), 0.5, 3.0, ((0, 32),))
    up_weight = bell_draw(splits[11], (D, FF), D ** -0.5, 0.21875, ((0, 32),))
    up_bias = bell_draw(splits[12], (FF,), 0.5, 3.0, ((0, 32),))
    down_weight = bell_draw(splits[13], (FF, D), FF ** -0.5, 0.109375, ((0, 32),))
    down_bias = bell_draw(splits[14], (D,), 0.5, 3.0, ((0, 32),))
    second_gain = jnp.clip(1.0 + 0.18 * jax.random.normal(splits[15], (D,), jnp.float32), 0.099609375, 1.8984375).astype(jnp.bfloat16)
    second_shift = bell_draw(splits[16], (D,), 0.5, 3.0, ((0, 32),))
    cotangent = heavy_noise(splits[17], (TOKENS, D), 1.0, 6.0, ((0, 32),), (0, 1, 32, 2.75))
    return {"tokens": tokens, "seq_lengths": seq_lengths, "query_weight": query_weight, "query_bias": query_bias, "key_weight": key_weight, "value_weight": value_weight, "value_bias": value_bias, "output_weight": output_weight, "output_bias": output_bias, "first_gain": first_gain, "first_shift": first_shift, "up_weight": up_weight, "up_bias": up_bias, "down_weight": down_weight, "down_bias": down_bias, "second_gain": second_gain, "second_shift": second_shift, "cotangent": cotangent}


@jax.custom_vjp
def low(v):
    return lax.optimization_barrier(v.astype(jnp.bfloat16)).astype(jnp.float32)

@jax.custom_vjp
def low_back(v):
    return v

def low_keep(v):
    return (low(v), None)

def low_pass(kept, grad):
    return (grad,)

def back_keep(v):
    return (v, None)

def back_low(kept, grad):
    return (low(grad),)
low.defvjp(low_keep, low_pass)
low_back.defvjp(back_keep, back_low)
HIGH = lax.Precision.HIGHEST
epsilon = 1e-05
neg_fill = -1e+30

def matmul(left, right):
    return jnp.dot(left, right, precision=HIGH, preferred_element_type=jnp.float32)

def segments(lengths):
    bounds = jnp.cumsum(lengths, dtype=jnp.int32)
    places = jnp.arange(MBLEN, dtype=jnp.int32)
    labels = lax.optimization_barrier(jnp.sum((places[:, None] >= bounds[None, :]).astype(jnp.int32), axis=1))
    live = (places < bounds[-1]).astype(jnp.float32)
    return (labels[:, None] == labels[None, :], live)

def layer_norm(rows, gain, shift):
    center = rows - lax.optimization_barrier(jnp.mean(rows, axis=-1, keepdims=True))
    scale = lax.rsqrt(lax.optimization_barrier(jnp.mean(center * center, axis=-1, keepdims=True)) + epsilon)
    return center * scale * gain + shift

def attend_pair(query, keys, values, same, index):
    query_pair = lax.dynamic_slice_in_dim(query, 2 * index, 2, 1)
    keys_pair = lax.dynamic_slice_in_dim(keys, 2 * index, 2, 1)
    values_pair = lax.dynamic_slice_in_dim(values, 2 * index, 2, 1)
    scores = jnp.einsum('qhd,khd->hqk', query_pair, keys_pair, precision=HIGH) * HD ** (-0.5)
    scores = jnp.where(same[None], low_back(scores), neg_fill)
    shares = jax.nn.softmax(scores, axis=-1)
    return jnp.einsum('hqk,khd->qhd', low(shares), values_pair, precision=HIGH)

def slot_forward(rows, lengths, params):
    query_weight, query_bias, key_weight, value_weight, value_bias, output_weight, output_bias, first_gain, first_shift, up_weight, up_bias, down_weight, down_bias, second_gain, second_shift = params
    same, live = segments(lengths)
    query = low_back(low(matmul(rows, query_weight) + query_bias)).reshape(MBLEN, H, HD)
    keys = low_back(low(matmul(rows, key_weight))).reshape(MBLEN, H, HD)
    values = low_back(low(matmul(rows, value_weight) + value_bias)).reshape(MBLEN, H, HD)
    pair_step = jax.checkpoint(attend_pair)
    mixed = lax.map(lambda index: pair_step(query, keys, values, same, index), jnp.arange(H // 2, dtype=jnp.int32))
    attended = low_back(low(jnp.transpose(mixed, (1, 0, 2, 3)).reshape(MBLEN, D)))
    branch = low_back(matmul(attended, output_weight) + output_bias)
    hidden = layer_norm(rows + branch, first_gain, first_shift)
    upward = low_back(matmul(low(hidden), up_weight) + up_bias)
    active = jax.nn.gelu(upward, approximate=False)
    feed = low_back(matmul(low(active), down_weight) + down_bias)
    return layer_norm(hidden + feed, second_gain, second_shift) * live[:, None]

def reference(tokens, seq_lengths, query_weight, query_bias, key_weight, value_weight, value_bias, output_weight, output_bias, first_gain, first_shift, up_weight, up_bias, down_weight, down_bias, second_gain, second_shift, cotangent):
    slots = seq_lengths.shape[0] * seq_lengths.shape[1]
    lengths_all = seq_lengths.reshape(slots, PACK)
    inputs = tokens.astype(jnp.float32).reshape(slots, MBLEN, D)
    params = tuple((piece.astype(jnp.float32) for piece in (query_weight, query_bias, key_weight, value_weight, value_bias, output_weight, output_bias, first_gain, first_shift, up_weight, up_bias, down_weight, down_bias, second_gain, second_shift)))

    def forward(block_inputs, weights):

        def step(carry, item):
            return (carry, jax.checkpoint(slot_forward)(item[0], item[1], weights))
        unused, results = lax.scan(step, None, (block_inputs, lengths_all))
        return results
    results, pullback = jax.vjp(forward, inputs, params)
    token_back, weight_back = pullback(cotangent.astype(jnp.float32).reshape(slots, MBLEN, D))
    return (results.reshape(TOKENS, D).astype(jnp.bfloat16), token_back.reshape(TOKENS, D), weight_back[0], weight_back[1], weight_back[2], weight_back[3], weight_back[4], weight_back[5], weight_back[6], weight_back[7], weight_back[8], weight_back[9], weight_back[10], weight_back[11], weight_back[12], weight_back[13], weight_back[14])
```

```python
import functools
import math

import jax
import jax.numpy as jnp
from jax import lax
from jax.experimental import pallas as pl
from jax.experimental.pallas import tpu as pltpu
from jax.sharding import PartitionSpec as P

HD = 64
LANES = 128
BLOCK = 256

epsilon = 1e-05
neg_fill = -1e30


def normalize(rows):
    center = rows - jnp.mean(rows, axis=-1, keepdims=True)
    scale = lax.rsqrt(jnp.mean(center * center, axis=-1, keepdims=True) + epsilon)
    return (center * scale, scale)


def norm_back(incoming, normed, scale):
    return scale * (
        incoming
        - jnp.mean(incoming, axis=-1, keepdims=True)
        - normed * jnp.mean(incoming * normed, axis=-1, keepdims=True)
    )


def rows_outer(left, right):
    out = jnp.einsum("ti,tj->ij", left, right, preferred_element_type=jnp.float32)
    return out.astype(jnp.bfloat16)


def times_transposed(left, right):
    return jnp.einsum("tj,ij->ti", left, right, preferred_element_type=jnp.float32)


def nt(left, right):
    return lax.dot_general(
        left, right, (((1,), (1,)), ((), ())), preferred_element_type=jnp.float32
    )


def three_parts(value):
    high = value.astype(jnp.bfloat16).astype(jnp.float32)
    rest = value - high
    middle = rest.astype(jnp.bfloat16).astype(jnp.float32)
    return (high, middle, rest - middle)


def forward_kernel(q_ref, k_ref, v_ref, mq_ref, mk_ref, out_ref, aug_ref):
    length = q_ref.shape[0]
    lane = lax.broadcasted_iota(jnp.int32, (length, LANES), 1)
    low_half = lane < HD
    query = q_ref[...] * jnp.asarray(HD**-0.5, jnp.bfloat16)
    keys, values = k_ref[...], v_ref[...]
    mq, mk = mq_ref[...], mk_ref[...]
    ones = jnp.ones_like(values)
    operands = []
    for head in range(2):
        mine = low_half if head == 0 else jnp.logical_not(low_half)
        operands.append(
            (
                jnp.where(mine, query, mq),
                jnp.where(mine, keys, mk),
                jnp.where(mine, values, ones),
            )
        )
    lane = lane[:BLOCK]
    low_half = low_half[:BLOCK]
    spot = lane % HD
    for start in range(0, length, BLOCK):
        mixed, logs = [], []
        for head in range(2):
            q_aug, k_aug, v_aug = operands[head]
            scores = nt(q_aug[start : start + BLOCK], k_aug)
            top = jnp.max(scores, axis=-1, keepdims=True)
            raised = jnp.exp(scores - top).astype(jnp.bfloat16)
            both = jnp.dot(raised, v_aug, preferred_element_type=jnp.float32)
            mixed.append(both / pltpu.roll(both, HD, 1))
            logs.append((top, both))
        out_ref[start : start + BLOCK, :] = jnp.where(low_half, mixed[0], mixed[1]).astype(
            jnp.bfloat16
        )
        total = jnp.where(low_half, logs[1][1], logs[0][1])
        top = jnp.where(low_half, logs[1][0], logs[0][0])
        high, middle, rest = three_parts(top + jnp.log(total))
        aug = jnp.where(
            spot == 8,
            high,
            jnp.where(
                spot == 9,
                middle,
                jnp.where(spot == 10, rest, mq[start : start + BLOCK].astype(jnp.float32)),
            ),
        )
        aug_ref[start : start + BLOCK, :] = aug.astype(jnp.bfloat16)


def backward_kernel(q_ref, k_ref, v_ref, aug_ref, mk_ref, o_ref, up_ref, dq_ref, dk_ref, dv_ref):
    length = q_ref.shape[0]
    scale = HD**-0.5
    lane = lax.broadcasted_iota(jnp.int32, (length, LANES), 1)
    low_half = lane < HD
    spot = lane % HD
    query = q_ref[...] * jnp.asarray(scale, jnp.bfloat16)
    keys, values, upstream = k_ref[...], v_ref[...], up_ref[...]
    aug, mk = aug_ref[...], mk_ref[...]
    product = upstream.astype(jnp.float32) * o_ref[...].astype(jnp.float32)
    zero = jnp.zeros_like(product)
    inner_low = jnp.sum(jnp.where(low_half, product, zero), axis=-1, keepdims=True)
    inner_high = jnp.sum(jnp.where(low_half, zero, product), axis=-1, keepdims=True)
    high, middle, rest = three_parts(jnp.where(low_half, inner_high, inner_low))
    up_aug = jnp.where(
        spot == 8, high, jnp.where(spot == 9, middle, jnp.where(spot == 10, rest, zero))
    ).astype(jnp.bfloat16)
    minus = jnp.where((spot >= 8) & (spot <= 10), -1.0, zero).astype(jnp.bfloat16)
    keys_turned = keys.astype(jnp.float32).T.astype(jnp.bfloat16)
    operands = []
    for head in range(2):
        mine = low_half if head == 0 else jnp.logical_not(low_half)
        operands.append(
            (
                jnp.where(mine, query, aug),
                jnp.where(mine, keys, mk),
                jnp.where(mine, upstream, up_aug),
                jnp.where(mine, values, minus),
            )
        )
    small_half = low_half[:BLOCK]
    turned = [None, None]
    for start in range(0, length, BLOCK):
        block = slice(start, start + BLOCK)
        key_parts, value_parts = [], []
        for head in range(2):
            q_aug, k_aug, u_aug, v_aug = operands[head]
            shares = jnp.exp(nt(k_aug[block], q_aug))
            score_back = (shares * nt(v_aug[block], u_aug)).astype(jnp.bfloat16)
            value_parts.append(
                jnp.dot(shares.astype(jnp.bfloat16), upstream, preferred_element_type=jnp.float32)
            )
            key_parts.append(jnp.dot(score_back, query, preferred_element_type=jnp.float32))
            part = jnp.dot(
                keys_turned[head * HD : (head + 1) * HD, block],
                score_back,
                preferred_element_type=jnp.float32,
            )
            turned[head] = part if turned[head] is None else turned[head] + part
        dk_ref[block, :] = jnp.where(small_half, key_parts[0], key_parts[1]).astype(jnp.bfloat16)
        dv_ref[block, :] = jnp.where(small_half, value_parts[0], value_parts[1]).astype(
            jnp.bfloat16
        )
    dq_ref[...] = (jnp.concatenate(turned, axis=0).T * scale).astype(jnp.bfloat16)


def attention_specs(length):
    wide = pl.BlockSpec((length, LANES), lambda slot, pair: (slot, pair))
    single = pl.BlockSpec((length, LANES), lambda slot, pair: (slot, 0))
    return wide, single


def attend_forward(query, keys, values, mq, mk, length):
    rows, width = query.shape
    wide, single = attention_specs(length)
    shape = jax.ShapeDtypeStruct((rows, width), jnp.bfloat16)
    return pl.pallas_call(
        forward_kernel,
        grid=(rows // length, width // LANES),
        in_specs=[wide, wide, wide, single, single],
        out_specs=[wide, wide],
        out_shape=[shape, shape],
        compiler_params=pltpu.CompilerParams(vmem_limit_bytes=48 * 2**20),
        cost_estimate=pl.CostEstimate(
            flops=8 * rows * length * width,
            bytes_accessed=10 * rows * width,
            transcendentals=rows * length * width // HD,
        ),
    )(query, keys, values, mq, mk)


def attend_backward(query, keys, values, aug, mk, attended, upstream, length):
    rows, width = query.shape
    wide, single = attention_specs(length)
    shape = jax.ShapeDtypeStruct((rows, width), jnp.bfloat16)
    return pl.pallas_call(
        backward_kernel,
        grid=(rows // length, width // LANES),
        in_specs=[wide, wide, wide, wide, single, wide, wide],
        out_specs=[wide, wide, wide],
        out_shape=[shape, shape, shape],
        compiler_params=pltpu.CompilerParams(vmem_limit_bytes=48 * 2**20),
        cost_estimate=pl.CostEstimate(
            flops=20 * rows * length * width,
            bytes_accessed=18 * rows * width,
            transcendentals=rows * length * width // HD,
        ),
    )(query, keys, values, aug, mk, attended, upstream)


def slot_masks(lengths, length):
    bounds = jnp.cumsum(lengths, axis=1, dtype=jnp.int32)
    places = jnp.arange(length, dtype=jnp.int32)
    past = (places[None, :, None] >= bounds[:, None, :]).astype(jnp.int32)
    labels = jnp.sum(past, axis=2).reshape(-1)
    live = (places[None, :] < bounds[:, -1:]).astype(jnp.float32).reshape(-1)
    spot = jnp.arange(LANES, dtype=jnp.int32)[None, :] % HD
    kinds = lengths.shape[1] + 1
    hit = spot == labels[:, None]
    mq = jnp.where(hit, 1.0, 0.0).astype(jnp.bfloat16)
    mk = jnp.where((spot < kinds) & jnp.logical_not(hit), neg_fill, 0.0)
    mk = jnp.where((spot >= 8) & (spot <= 10), -1.0, mk).astype(jnp.bfloat16)
    return live, mq, mk


def scatter_sum(full, width, order):
    bits = width.bit_length() - 1
    chunk = (full.shape[0] // width,) + full.shape[1:]
    data = full.reshape((2,) * bits + chunk)
    me = lax.axis_index("fsdp")
    axes = list(range(bits - 1, -1, -1))
    for bit in order:
        axis = axes.index(bit)
        axes.pop(axis)
        mine = lax.rem(lax.div(me, 1 << bit), 2)
        send = lax.dynamic_index_in_dim(data, 1 - mine, axis, keepdims=False)
        keep = lax.dynamic_index_in_dim(data, mine, axis, keepdims=False)
        pairs = [(device, device ^ (1 << bit)) for device in range(width)]
        came = lax.ppermute(send, "fsdp", pairs)
        data = (keep.astype(jnp.float32) + came.astype(jnp.float32)).astype(full.dtype)
    return data


def orders(width):
    bits = width.bit_length() - 1
    rest = list(range(1, bits))
    return [[0] + rest[turn:] + rest[:turn] for turn in range(max(1, len(rest)))]


def on_device(
    tokens,
    seq_lengths,
    query_weight,
    query_bias,
    key_weight,
    value_weight,
    value_bias,
    output_weight,
    output_bias,
    first_gain,
    first_shift,
    up_weight,
    up_bias,
    down_weight,
    down_bias,
    second_gain,
    second_shift,
    cotangent,
):
    width = lax.axis_size("fsdp")
    length = tokens.shape[0] // seq_lengths.shape[1]
    model = tokens.shape[1]
    hidden_units = up_weight.shape[1]
    gather = functools.partial(lax.all_gather, axis_name="fsdp", axis=0, tiled=False)

    vectors = (
        query_bias,
        value_bias,
        output_bias,
        first_gain,
        first_shift,
        up_bias,
        down_bias,
        second_gain,
        second_shift,
    )
    sizes = [piece.shape[0] for piece in vectors]
    flat = jnp.concatenate(vectors)
    flat_rows = -(-flat.shape[0] // model)
    flat = jnp.pad(flat, (0, flat_rows * model - flat.shape[0])).reshape(flat_rows, model)
    part = query_weight.shape[0]
    early = gather(jnp.concatenate([query_weight, key_weight, value_weight, flat], axis=0))
    late = gather(
        jnp.concatenate([output_weight, down_weight, up_weight.reshape(-1, model)], axis=0)
    )

    full_vectors = []
    gathered_flat = early[:, 3 * part :].reshape(width, -1)
    start = 0
    for size in sizes:
        full_vectors.append(
            gathered_flat[:, start : start + size].reshape(-1).astype(jnp.float32)
        )
        start += size
    (
        query_bias,
        value_bias,
        output_bias,
        first_gain,
        first_shift,
        up_bias,
        down_bias,
        second_gain,
        second_shift,
    ) = full_vectors
    query_weight = early[:, :part].reshape(model, model)
    key_weight = early[:, part : 2 * part].reshape(model, model)
    value_weight = early[:, 2 * part : 3 * part].reshape(model, model)
    down_part = down_weight.shape[0]
    output_weight = late[:, :part].reshape(model, model)
    down_weight = late[:, part : part + down_part].reshape(hidden_units, model)
    up_weight = late[:, part + down_part :].reshape(model, hidden_units)

    live, mq, mk = slot_masks(seq_lengths[0], length)
    live = live[:, None]
    query = (jnp.dot(tokens, query_weight, preferred_element_type=jnp.float32) + query_bias).astype(
        jnp.bfloat16
    )
    keys = jnp.dot(tokens, key_weight, preferred_element_type=jnp.float32).astype(jnp.bfloat16)
    values = (
        jnp.dot(tokens, value_weight, preferred_element_type=jnp.float32) + value_bias
    ).astype(jnp.bfloat16)
    attended, aug = attend_forward(query, keys, values, mq, mk, length)
    first = (
        tokens.astype(jnp.float32)
        + jnp.dot(attended, output_weight, preferred_element_type=jnp.float32)
        + output_bias
    )
    normed_one, scale_one = normalize(first)
    hidden = normed_one * first_gain + first_shift
    hidden_low = hidden.astype(jnp.bfloat16)
    upward = jnp.dot(hidden_low, up_weight, preferred_element_type=jnp.float32) + up_bias
    share = 0.5 * (1.0 + lax.erf(upward * (1.0 / math.sqrt(2.0))))
    active = (upward * share).astype(jnp.bfloat16)
    slope = (
        share + upward * jnp.exp(-0.5 * upward * upward) * (1.0 / math.sqrt(2.0 * math.pi))
    ).astype(jnp.bfloat16)
    second = hidden + jnp.dot(active, down_weight, preferred_element_type=jnp.float32) + down_bias
    normed_two, scale_two = normalize(second)
    layer_output = ((normed_two * second_gain + second_shift) * live).astype(jnp.bfloat16)

    upstream = cotangent.astype(jnp.float32) * live
    second_shift_back = jnp.sum(upstream, axis=0)
    second_gain_back = jnp.sum(upstream * normed_two, axis=0)
    second_back = norm_back(upstream * second_gain, normed_two, scale_two)
    mix_low = second_back.astype(jnp.bfloat16)
    ways = orders(width)
    down_weight_back = scatter_sum(rows_outer(active, mix_low), width, ways[0])
    down_bias_back = jnp.sum(mix_low.astype(jnp.float32), axis=0)
    up_low = (times_transposed(mix_low, down_weight) * slope).astype(jnp.bfloat16)
    up_weight_back = scatter_sum(rows_outer(hidden_low, up_low), width, ways[1 % len(ways)])
    up_bias_back = jnp.sum(up_low.astype(jnp.float32), axis=0)
    hidden_back = second_back + times_transposed(up_low, up_weight)
    first_shift_back = jnp.sum(hidden_back, axis=0)
    first_gain_back = jnp.sum(hidden_back * normed_one, axis=0)
    first_back = norm_back(hidden_back * first_gain, normed_one, scale_one)
    out_low = first_back.astype(jnp.bfloat16)
    output_weight_back = scatter_sum(rows_outer(attended, out_low), width, ways[2 % len(ways)])
    output_bias_back = jnp.sum(out_low.astype(jnp.float32), axis=0)
    attended_back = times_transposed(out_low, output_weight).astype(jnp.bfloat16)
    query_low, key_low, value_low = attend_backward(
        query, keys, values, aug, mk, attended, attended_back, length
    )
    query_weight_back = scatter_sum(rows_outer(tokens, query_low), width, ways[0])
    key_weight_back = scatter_sum(rows_outer(tokens, key_low), width, ways[1 % len(ways)])
    value_weight_back = scatter_sum(rows_outer(tokens, value_low), width, ways[2 % len(ways)])
    query_bias_back = jnp.sum(query_low.astype(jnp.float32), axis=0)
    value_bias_back = jnp.sum(value_low.astype(jnp.float32), axis=0)
    token_gradient = (
        first_back
        + times_transposed(query_low, query_weight)
        + times_transposed(key_low, key_weight)
        + times_transposed(value_low, value_weight)
    )
    vector_backs = (
        query_bias_back,
        value_bias_back,
        output_bias_back,
        first_gain_back,
        first_shift_back,
        up_bias_back,
        down_bias_back,
        second_gain_back,
        second_shift_back,
    )
    packed = jnp.concatenate([piece.reshape(width, -1) for piece in vector_backs], axis=1)
    summed = scatter_sum(packed, width, ways[0]).reshape(-1)
    split = []
    start = 0
    for size in sizes:
        split.append(summed[start : start + size])
        start += size
    (
        query_bias_back,
        value_bias_back,
        output_bias_back,
        first_gain_back,
        first_shift_back,
        up_bias_back,
        down_bias_back,
        second_gain_back,
        second_shift_back,
    ) = split
    return (
        layer_output,
        token_gradient,
        query_weight_back.astype(jnp.float32),
        query_bias_back,
        key_weight_back.astype(jnp.float32),
        value_weight_back.astype(jnp.float32),
        value_bias_back,
        output_weight_back.astype(jnp.float32),
        output_bias_back,
        first_gain_back,
        first_shift_back,
        up_weight_back.astype(jnp.float32),
        up_bias_back,
        down_weight_back.astype(jnp.float32),
        down_bias_back,
        second_gain_back,
        second_shift_back,
    )


def solution(mesh):
    rows, flat = P("fsdp", None), P("fsdp")
    return jax.shard_map(
        on_device,
        mesh=mesh,
        in_specs=(
            rows,
            P("fsdp", None, None),
            rows,
            flat,
            rows,
            rows,
            flat,
            rows,
            flat,
            flat,
            flat,
            rows,
            flat,
            rows,
            flat,
            flat,
            flat,
            rows,
        ),
        out_specs=(
            rows,
            rows,
            rows,
            flat,
            rows,
            rows,
            flat,
            rows,
            flat,
            flat,
            flat,
            rows,
            flat,
            rows,
            flat,
            flat,
            flat,
        ),
        check_vma=False,
    )
```
